256 devices in a mesh: seq: 32 (over z_lo, y, core), head: 8 (over z_hi, x).
Axes of the slice: x: 4, y: 4, z: 8 (z_hi: 2, z_lo: 4; z = z_hi * 4 + z_lo), core: 2. Of those that a mesh axis runs over, the one named last changes fastest.
Arguments:
- queries: bfloat16 [32768, 8192], P(('seq', 'head')), may hold values from -17 to 17
- keys: bfloat16 [32768, 1024], P(('seq', 'head')), may hold values from -17 to 17
- values: bfloat16 [32768, 1024], P(('seq', 'head')), may hold values from -6 to 6
- lengths: int32 [64], replicated, may hold values from 1 to 2048, 32768 in all
Outputs:
- attended: bfloat16 [32768, 8192], P(('seq', 'head'))
The draws below stay inside these ranges and needn't reach their ends.
Inputs may be any that keep to these rules, and one draw needn't show every extreme that they name: document lengths sum to 32768; the longest is exactly 2048.
All inputs are finite; a program needn't handle non-finite values.
Results may differ from the reference program's by a relative error of at most 0.0044.
Values may be sent and summed in bfloat16 or wider, within the bound.
A program may use at most 128 MiB of HBM per device.

```python
import math
import jax
import jax.numpy as jnp
import numpy as np
from jax import lax

H = 64
KVH = 8
DH = 128
REACH = 2
TOKENS = 32768
MOST = 2048
NDOCS = 64
N_SEQ = 32


def draw_queries(key, part):
    key = jax.random.fold_in(key, 1)
    base = jnp.clip(jax.random.normal(key, (TOKENS, H * DH), jnp.float32), -4.0, 4.0)
    return base.astype(jnp.bfloat16)


def draw_keys(key, part):
    key = jax.random.fold_in(key, 2)
    base = jnp.clip(jax.random.normal(key, (TOKENS, KVH * DH), jnp.float32), -4.0, 4.0)
    return base.astype(jnp.bfloat16)


def block_scale(stream_key, shape, shards, smallest, high):
    factor_of, own = 1.0, jax.random.fold_in(stream_key, 6)
    for dim, shards_of in shards:
        steps = jnp.exp(jax.random.uniform(jax.random.fold_in(own, dim), (shards_of,), jnp.float32, smallest / len(shards), high / len(shards)))
        factor_of = factor_of * jnp.repeat(steps, shape[dim] // shards_of).reshape([-1 if axis == dim else 1 for axis in range(len(shape))])
    return factor_of


def split_up(amount, total, limit, slope):
    weights = [(1 << 20) // math.isqrt(standing ** slope) + 1 for standing in range(2, amount + 1)]
    spare, given = total - limit - (amount - 1), [1] * (amount - 1)
    while spare > 0:
        free = [i for i in range(amount - 1) if given[i] < limit]
        mass, remaining = sum([weights[i] for i in free]), spare
        for i in free:
            addition = min(limit - given[i], max(1, remaining * weights[i] // mass), spare)
            given[i] = given[i] + addition
            spare = spare - addition
    return np.array([limit] + given)


def uneven(stream_key, number_of, total, bound, slope):
    if number_of == 2:
        one = jax.random.randint(stream_key, (), max(1, total - bound), min(bound, total - 1) + 1)
        return jnp.stack([one, total - one])
    tallies = jnp.asarray(split_up(number_of, total, bound, slope), jnp.int32)
    couples = (number_of - 1) // 2
    giver, receiver = tallies[1:1 + 2 * couples:2], tallies[2:2 + 2 * couples:2]
    slack = jnp.minimum(giver - 1, bound - receiver)
    passed = jax.random.randint(jax.random.fold_in(stream_key, 1), (couples,), 0, 1 << 20) % (slack + 1)
    tallies = tallies.at[1:1 + 2 * couples:2].set(giver - passed).at[2:2 + 2 * couples:2].set(receiver + passed)
    return tallies[jax.random.permutation(jax.random.fold_in(stream_key, 2), number_of)]


def normal_values(key, shape, scale, bound, shards=(), kind=jnp.bfloat16):
    array = scale * jax.random.normal(key, shape, jnp.float32)
    if shards:
        array = array * block_scale(key, shape, shards, -0.22, 0.18)
    return jnp.clip(array, -bound, bound).astype(kind)


def setup_inputs(seed: int = 0) -> dict:
    streams_of = jax.random.split(jax.random.key(seed), 5)
    queries = draw_queries(jax.random.fold_in(streams_of[4], 71), 0)
    keys = draw_keys(jax.random.fold_in(streams_of[4], 71), 0)
    values = normal_values(streams_of[2], (TOKENS, KVH * DH), 1.0, 6.0, ((0, 256),))
    lengths = uneven(streams_of[3], NDOCS, TOKENS, MOST, 2).astype(jnp.int32)
    return {"queries": queries, "keys": keys, "values": values, "lengths": lengths}


def reference(queries, keys, values, lengths):
    tokens = queries.shape[0]
    shard = tokens // N_SEQ
    back = REACH * shard
    group = H // KVH
    scale = 1.0 / (DH ** 0.5)
    ends = jnp.cumsum(lengths).astype(jnp.int32)
    places = jnp.arange(tokens, dtype=jnp.int32)
    document = jnp.sum((ends[None, :] <= places[:, None]).astype(jnp.int32), axis=1)
    query_all = queries.reshape(tokens, KVH, group, DH)
    key_pad = jnp.concatenate([jnp.zeros((back, KVH * DH), keys.dtype), keys], axis=0).reshape(-1, KVH, DH)
    value_pad = jnp.concatenate([jnp.zeros((back, KVH * DH), values.dtype), values], axis=0).reshape(-1, KVH, DH)
    doc_pad = jnp.concatenate([jnp.full((back,), -1, jnp.int32), document])

    def one_shard(index):
        start = (index * shard).astype(jnp.int32)
        query_block = lax.dynamic_slice_in_dim(query_all, start, shard, 0)
        key_block = lax.dynamic_slice_in_dim(key_pad, start, back + shard, 0)
        value_block = lax.dynamic_slice_in_dim(value_pad, start, back + shard, 0)
        query_doc = lax.dynamic_slice_in_dim(document, start, shard, 0)
        key_doc = lax.dynamic_slice_in_dim(doc_pad, start, back + shard, 0)
        query_pos = start + jnp.arange(shard, dtype=jnp.int32)
        key_pos = start - back + jnp.arange(back + shard, dtype=jnp.int32)
        live = (query_doc[:, None] == key_doc[None, :]) & (key_pos[None, :] <= query_pos[:, None])

        def one_head(head):
            qh = lax.dynamic_index_in_dim(query_block, head, 1, keepdims=False).astype(jnp.float32)
            kh = lax.dynamic_index_in_dim(key_block, head, 1, keepdims=False).astype(jnp.float32)
            vh = lax.dynamic_index_in_dim(value_block, head, 1, keepdims=False).astype(jnp.float32)
            scores = jnp.einsum('qgd,kd->gqk', qh, kh) * scale
            scores = jnp.where(live[None], scores, -1e30)
            top = jnp.max(scores, axis=2, keepdims=True)
            weights = jnp.where(live[None], jnp.exp(scores - top), 0.0)
            total = jnp.sum(weights, axis=2)
            rounded = weights.astype(jnp.bfloat16).astype(jnp.float32)
            mixed = jnp.einsum('gqk,kd->qgd', rounded, vh)
            return (mixed / jnp.transpose(total)[:, :, None]).astype(jnp.bfloat16)

        heads_out = lax.map(one_head, jnp.arange(KVH, dtype=jnp.int32))
        return jnp.transpose(heads_out, (1, 0, 2, 3))

    shards_out = lax.map(one_shard, jnp.arange(N_SEQ, dtype=jnp.int32))
    return shards_out.reshape(tokens, H * DH)
```

```python
import functools
import math

import jax
import jax.numpy as jnp
from jax import lax
from jax.experimental import pallas as pl
from jax.experimental.pallas import tpu as pltpu
from jax.sharding import PartitionSpec as P

H, KVH, DH = 64, 8, 128
GROUP = H // KVH
TOK = 128
ROWS = GROUP * TOK
BIG = 1e30
RATE = math.log2(math.e) / math.sqrt(DH)
MESH = pl.DeviceIdType.MESH


class Place:
    def __init__(self):
        self.s, self.h = s, h = lax.axis_index("seq"), lax.axis_index("head")
        self.core = lax.rem(s, 2)
        self.x, self.z = lax.rem(h, 4), h // 4
        self.own, self.other = self.z * 4, 4 - self.z * 4
        self.xl, self.xr, self.xo = (lax.rem(self.x + d, 4) for d in (3, 1, 2))
        self.right, self.left = (s, self.own + self.xr), (s, self.own + self.xl)
        self.far = (s, self.other + self.x)
        self.twin = (s + 1 - 2 * self.core, h)
        self.later, self.before = (s + 2, h), (s - 2, h)
        self.has_later, self.has_before = s < 30, s >= 2


def when(cond, action):
    if cond is None:
        action()
    else:
        pl.when(cond)(action)


def spread(column, width):
    return jnp.concatenate([column] * (width // 128), axis=1)


def kernel(
    q_hbm, k_hbm, v_hbm, len_ref, o_hbm,
    kv, q_raw, qa, km, acc, top, tot, out, bounds,
    load_sem, out_sem, ss_x, ss_c, ss_y, ss_z, rs,
):
    p = Place()
    s, h, core, x = p.s, p.h, p.core, p.x
    loads = [
        pltpu.make_async_copy(k_hbm, kv.at[0, h, 0], load_sem.at[0]),
        pltpu.make_async_copy(v_hbm, kv.at[0, h, 1], load_sem.at[1]),
        pltpu.make_async_copy(q_hbm, q_raw, load_sem.at[2]),
    ]
    for load in loads:
        load.start()

    barrier = pltpu.get_barrier_semaphore()

    def greet(device):
        pl.semaphore_signal(barrier, inc=1, device_id=device, device_id_type=MESH)

    for device in (p.left, p.right, p.far, p.twin):
        greet(device)
    when(p.has_before, lambda: greet(p.before))
    when(p.has_later, lambda: greet(p.later))

    @pl.when(s < 2)
    def _():
        kv[2] = jnp.zeros(kv.shape[1:], kv.dtype)

    @pl.when(s == 0)
    def _():
        kv[1] = jnp.zeros(kv.shape[1:], kv.dtype)

    pl.semaphore_wait(barrier, 4 + p.has_before.astype(jnp.int32) + p.has_later.astype(jnp.int32))
    loads[0].wait()
    loads[1].wait()

    sends = []

    def send(cond, src, dst, sem, device):
        copy = pltpu.make_async_remote_copy(
            src_ref=kv.at[src], dst_ref=kv.at[dst], send_sem=sem, recv_sem=rs.at[dst],
            device_id=device, device_id_type=MESH,
        )
        when(cond, copy.start)
        sends.append((cond, copy))

    def arrived(cond, where):
        copy = pltpu.make_async_remote_copy(
            src_ref=kv.at[where], dst_ref=kv.at[where], send_sem=ss_z.at[0], recv_sem=rs.at[where],
            device_id=p.right, device_id_type=MESH,
        )
        when(cond, copy.wait_recv)

    def modes(row, other):
        gathers = core == row // 2
        on = (s >= 2) if row == 2 else (s >= 0)
        if other:
            return on & (gathers | (core == p.z)), None, on & gathers
        return on & gathers, on & jnp.logical_not(gathers), on & gathers

    def begin(phase, row, other):
        full, part, gathers = modes(row, other)
        slot = (p.other if other else p.own) + x
        to_right, to_left = full, full
        if part is not None:
            if row == 0:
                to_right, to_left = full | part & (x < 3), full | part & (x == 0)
            else:
                to_right, to_left = full | part & (x == 3), full | part & (x > 0)
        for t in range(2):
            here = (row, slot, t)
            send(to_right, here, here, ss_x.at[phase, t], p.right)
            send(to_left, here, here, ss_x.at[phase, 2 + t], p.left)
            send(gathers, here, (1, slot, t), ss_c.at[slot, t], p.twin)

    def middle(phase, row, other):
        full, part, gathers = modes(row, other)
        base = p.other if other else p.own
        sl, sr = base + p.xl, base + p.xr
        inner = (x == 1) | (x == 2)
        from_left, from_right = full, full
        on_right, on_left = [full, None], [None, full]
        if part is not None:
            if row == 0:
                from_left, from_right = full | part & (x > 0), full | part & (x == 3)
                on_right = [full | part & inner, part & inner]
            else:
                from_left, from_right = full | part & (x == 0), full | part & (x < 3)
                on_left = [part & inner, full | part & inner]
        for t in range(2):
            here = (row, sl, t)
            arrived(from_left, here)
            if on_right[t] is not None:
                send(on_right[t], here, here, ss_x.at[phase, 4 + t], p.right)
            send(gathers, here, (1, sl, t), ss_c.at[sl, t], p.twin)
            here = (row, sr, t)
            arrived(from_right, here)
            if on_left[t] is not None:
                send(on_left[t], here, here, ss_x.at[phase, 6 + t], p.left)
            send(gathers, here, (1, sr, t), ss_c.at[sr, t], p.twin)

    def end(phase, row, other):
        full, part, gathers = modes(row, other)
        so = (p.other if other else p.own) + p.xo
        got = full
        if part is not None:
            got = full | part & ((x >= 2) if row == 0 else (x < 2))
        for t in range(2):
            here = (row, so, t)
            arrived(got, here)
            send(gathers, here, (1, so, t), ss_c.at[so, t], p.twin)

    def twin_sent(slots):
        for slot in slots:
            for t in range(2):
                arrived(s >= 1, (1, slot, t))

    def block_mask(row, slot):
        pos = ((s - row) * 8 + slot) * TOK + lax.broadcasted_iota(jnp.int32, (TOK, DH), 0)
        starts, ends = bounds[0:1, :], bounds[1:2, :]
        return jnp.where((pos >= starts) & (pos < ends), 0.0, -BIG).astype(jnp.bfloat16)

    def attend(blocks, first=False, last=False):
        count = len(blocks)
        width = count * TOK
        for i, (row, slot) in enumerate(blocks):
            km[i * TOK:(i + 1) * TOK, :] = block_mask(row, slot)

        def one_head(j, carry):
            lanes = pl.ds(pl.multiple_of(j * DH, DH), DH)
            keys = jnp.concatenate([kv[row, slot, 0, :, lanes] for row, slot in blocks], axis=0)
            keys = jnp.concatenate([keys, km[0:width, :]], axis=1)
            values = jnp.concatenate([kv[row, slot, 1, :, lanes] for row, slot in blocks], axis=0)
            values = jnp.concatenate([values, jnp.ones((width, DH), jnp.bfloat16)], axis=1)
            for part in range(ROWS // CHUNK):
                rows = pl.ds(part * CHUNK, CHUNK)
                scores = lax.dot_general(
                    qa[j, rows, :], keys, (((1,), (1,)), ((), ())), preferred_element_type=jnp.float32
                )
                if first:
                    token = lax.broadcasted_iota(jnp.int32, (CHUNK, width), 0) & (TOK - 1)
                    key = lax.broadcasted_iota(jnp.int32, (CHUNK, width), 1)
                    scores = jnp.where(key <= token, scores, -BIG)
                best = jnp.broadcast_to(jnp.max(scores, axis=1, keepdims=True), (CHUNK, DH))
                if not first:
                    old = top[j, rows, :]
                    best = jnp.maximum(best, old)
                weights = jnp.exp2((scores - spread(best, width)) * RATE).astype(jnp.bfloat16)
                both = jnp.dot(weights, values, preferred_element_type=jnp.float32)
                mixed, total = both[:, :DH], both[:, DH:]
                if not first:
                    factor = jnp.exp2((old - best) * RATE)
                    mixed = mixed + acc[j, rows, :] * factor
                    total = total + tot[j, rows, :] * factor
                if last:
                    done = (mixed / total).astype(jnp.bfloat16)
                    for g in range(CHUNK // TOK):
                        column = (j * GROUP + part * (CHUNK // TOK) + g) * DH
                        out[:, pl.ds(pl.multiple_of(column, DH), DH)] = done[g * TOK:(g + 1) * TOK]
                else:
                    top[j, rows, :] = best
                    acc[j, rows, :] = mixed
                    tot[j, rows, :] = total
            if last:
                columns = pl.ds(pl.multiple_of(j * GROUP * DH, DH), GROUP * DH)
                pltpu.make_async_copy(out.at[:, columns], o_hbm.at[:, columns], out_sem.at[j]).start()
            return carry

        lax.fori_loop(0, KVH, one_head, 0)

    far = p.other + x
    wanted = (core == 1) | (p.z == 0)
    for t in range(2):
        send(p.has_later, (0, h, t), (2, h, t), ss_y.at[0, t], p.later)
    for t in range(2):
        send(None, (0, h, t), (0, h, t), ss_z.at[t], p.far)
    begin(0, 0, False)

    lens = jnp.concatenate([len_ref[...], jnp.zeros((1, DH - len_ref.shape[1]), jnp.int32)], axis=1)
    lens = jnp.broadcast_to(lens, (8, DH))
    lane = lax.broadcasted_iota(jnp.int32, (8, DH), 1)
    ends = lens
    for step in (1, 2, 4, 8, 16, 32, 64):
        ends = ends + jnp.where(lane >= step, pltpu.roll(ends, step, 1), 0)
    bounds[0:1, :] = (ends - lens)[0:1]
    bounds[1:2, :] = ends[0:1]
    pos = (s * 8 + h) * TOK + lax.broadcasted_iota(jnp.int32, (TOK, DH), 0)
    member = jnp.where((pos >= bounds[0:1, :]) & (pos < bounds[1:2, :]), 1.0, 0.0).astype(jnp.bfloat16)
    loads[2].wait()

    def arrange(j, carry):
        for g in range(GROUP):
            column = pl.multiple_of((j * GROUP + g) * DH, DH)
            qa[j, g * TOK:(g + 1) * TOK, 0:DH] = q_raw[:, pl.ds(column, DH)]
            qa[j, g * TOK:(g + 1) * TOK, DH:2 * DH] = member
        return carry

    lax.fori_loop(0, KVH, arrange, 0)

    attend([(0, h)], first=True)
    middle(0, 0, False)
    for t in range(2):
        arrived(p.has_before, (2, h, t))
    begin(1, 2, False)
    end(0, 0, False)
    middle(1, 2, False)
    for t in range(2):
        arrived(None, (0, far, t))
    for t in range(2):
        send(p.has_later & wanted, (0, far, t), (2, far, t), ss_y.at[1, t], p.later)
    begin(2, 0, True)
    end(1, 2, False)

    def mixed_row(other_x):
        return jnp.where(other_x < x, 0, 2)

    own, other = p.own, p.other
    attend([(mixed_row(d), own + d) for d in (p.xl, p.xr, p.xo)] + [(2, h)])
    middle(2, 0, True)
    twin_sent([own + d for d in range(4)])
    attend([(1, own + d) for d in range(4)])
    end(2, 0, True)
    for t in range(2):
        arrived(p.has_before & wanted, (2, far, t))
    begin(3, 2, True)

    late_both = (core == 0) & (p.z == 0)
    row_b = jnp.where(p.z == 0, 2, 0)
    first_row = jnp.where((core == 0) & (p.z == 1), row_b, 1)
    second_row = jnp.where((core == 0) & (p.z == 1), 1, row_b)
    order = [x, p.xl, p.xr, p.xo]
    plain = [(first_row, d) for d in order] + [(second_row, d) for d in order]
    paired = [(row, d) for d in order for row in (first_row, second_row)]
    todo = [
        (jnp.where(late_both, a, c), other + jnp.where(late_both, b, d))
        for (a, b), (c, d) in zip(paired, plain)
    ]


    for t in range(2):
        arrived(s >= 1, (1, far, t))
    early = (core == 1) & (s >= 1)
    for d in order[1:]:
        for t in range(2):
            arrived(early, (1, other + d, t))
    attend(todo[0:2])
    middle(3, 2, True)
    late = (core == 0) & (s >= 1)
    for d in order[1:3]:
        for t in range(2):
            arrived(late, (1, other + d, t))
    attend(todo[2:4])
    attend(todo[4:6])
    end(3, 2, True)
    for t in range(2):
        arrived(late, (1, other + p.xo, t))
    attend(todo[6:8], last=True)

    for cond, copy in sends:
        when(cond, copy.wait_send)
    for j in range(KVH):
        columns = pl.ds(j * GROUP * DH, GROUP * DH)
        pltpu.make_async_copy(out.at[:, columns], o_hbm.at[:, columns], out_sem.at[j]).wait()


CHUNK = 256


def per_device(queries, keys, values, lengths):
    tok = queries.shape[0]
    f32, bf16, dma = jnp.float32, jnp.bfloat16, pltpu.SemaphoreType.DMA
    return pl.pallas_call(
        kernel,
        out_shape=jax.ShapeDtypeStruct(queries.shape, bf16),
        in_specs=[pl.BlockSpec(memory_space=pl.ANY)] * 3 + [pl.BlockSpec(memory_space=pltpu.VMEM)],
        out_specs=pl.BlockSpec(memory_space=pl.ANY),
        scratch_shapes=[
            pltpu.VMEM((3, 8, 2, tok, KVH * DH), bf16),
            pltpu.VMEM((tok, H * DH), bf16),
            pltpu.VMEM((KVH, ROWS, 2 * DH), bf16),
            pltpu.VMEM((4 * tok, DH), bf16),
            pltpu.VMEM((KVH, ROWS, DH), f32),
            pltpu.VMEM((KVH, ROWS, DH), f32),
            pltpu.VMEM((KVH, ROWS, DH), f32),
            pltpu.VMEM((tok, H * DH), bf16),
            pltpu.VMEM((8, DH), jnp.int32),
            dma((3,)), dma((KVH,)), dma((4, 8)), dma((8, 2)), dma((2, 2)), dma((2,)), dma((3, 8, 2)),
        ],
        compiler_params=pltpu.CompilerParams(
            collective_id=0, has_side_effects=True, vmem_limit_bytes=56 << 20
        ),
        name="attend",
    )(queries, keys, values, lengths.reshape(1, -1))


def solution(mesh):
    spec = P(("seq", "head"), None)
    return jax.shard_map(
        per_device, mesh=mesh, in_specs=(spec, spec, spec, P()), out_specs=spec, check_vma=False
    )
```

```python
import functools
import math

import jax
import jax.numpy as jnp
from jax import lax
from jax.experimental import pallas as pl
from jax.experimental.pallas import tpu as pltpu
from jax.sharding import PartitionSpec as P

H, KVH, DH = 64, 8, 128
GROUP = H // KVH
TOK = 128
ROWS = GROUP * TOK
BIG = 1e30
RATE = math.log2(math.e) / math.sqrt(DH)
MESH = pl.DeviceIdType.MESH


class Place:
    def __init__(self):
        self.s, self.h = s, h = lax.axis_index("seq"), lax.axis_index("head")
        self.core = lax.rem(s, 2)
        self.x, self.y, self.z = lax.rem(h, 4), lax.rem(s // 2, 4), h // 4
        self.own, self.other = self.z * 4, 4 - self.z * 4
        self.xl, self.xr, self.xo = (lax.rem(self.x + d, 4) for d in (3, 1, 2))
        self.right, self.left = (s, self.own + self.xr), (s, self.own + self.xl)
        self.far = (s, self.other + self.x)
        self.twin = (s + 1 - 2 * self.core, h)
        self.later, self.before = (s + 2, h), (s - 2, h)
        self.has_later, self.has_before = s < 30, s >= 2


def when(cond, action):
    if cond is None:
        action()
    else:
        pl.when(cond)(action)


def spread(column, width):
    return jnp.concatenate([column] * (width // 128), axis=1)


def kernel(
    q_hbm, k_hbm, v_hbm, len_ref, o_hbm,
    kv, q_raw, qa, km, acc, top, tot, out, bounds,
    load_sem, out_sem, ss_x, ss_c, ss_y, ss_z, rs,
):
    p = Place()
    s, h, core, x = p.s, p.h, p.core, p.x
    loads = [
        pltpu.make_async_copy(k_hbm, kv.at[0, h, 0], load_sem.at[0]),
        pltpu.make_async_copy(v_hbm, kv.at[0, h, 1], load_sem.at[1]),
        pltpu.make_async_copy(q_hbm, q_raw, load_sem.at[2]),
    ]
    for load in loads:
        load.start()

    barrier = pltpu.get_barrier_semaphore()

    def greet(device):
        pl.semaphore_signal(barrier, inc=1, device_id=device, device_id_type=MESH)

    for device in (p.left, p.right, p.far, p.twin):
        greet(device)
    when(p.has_before, lambda: greet(p.before))
    when(p.has_later, lambda: greet(p.later))

    @pl.when(s < 2)
    def _():
        kv[2] = jnp.zeros(kv.shape[1:], kv.dtype)

    @pl.when(s == 0)
    def _():
        kv[1] = jnp.zeros(kv.shape[1:], kv.dtype)

    pl.semaphore_wait(barrier, 4 + p.has_before.astype(jnp.int32) + p.has_later.astype(jnp.int32))
    sends = []

    def send(cond, src, dst, sem, device, now=None):
        copy = pltpu.make_async_remote_copy(
            src_ref=src if not isinstance(src, tuple) else kv.at[src], dst_ref=kv.at[dst], send_sem=sem, recv_sem=rs.at[dst],
            device_id=device, device_id_type=MESH,
        )
        when(cond if now is None else now, copy.start)
        sends.append((cond, copy))
        return copy

    def arrived(cond, where):
        copy = pltpu.make_async_remote_copy(
            src_ref=kv.at[where], dst_ref=kv.at[where], send_sem=ss_z.at[0], recv_sem=rs.at[where],
            device_id=p.right, device_id_type=MESH,
        )
        when(cond, copy.wait_recv)

    def modes(row, other):
        gathers = core == row // 2
        on = (s >= 2) if row == 2 else (s >= 0)
        if other:
            return on & (gathers | (core == p.z)), None, on & gathers
        return on & gathers, on & jnp.logical_not(gathers), on & gathers

    def begin(phase, row, other, t, source=None):
        full, part, gathers = modes(row, other)
        slot = (p.other if other else p.own) + x
        to_right, to_left = full, full
        if part is not None:
            if row == 0:
                to_right, to_left = full | part & (x < 3), full | part & (x == 0)
            else:
                to_right, to_left = full | part & (x == 3), full | part & (x > 0)
        here = (row, slot, t)
        source = here if source is None else source
        send(to_right, source, here, ss_x.at[phase, t], p.right)
        send(to_left, source, here, ss_x.at[phase, 2 + t], p.left)
        send(gathers, source, (1, slot, t), ss_c.at[slot, t], p.twin)

    def middle(phase, row, other):
        full, part, gathers = modes(row, other)
        base = p.other if other else p.own
        sl, sr = base + p.xl, base + p.xr
        inner = (x == 1) | (x == 2)
        from_left, from_right = full, full
        on_right, on_left = [full, None], [None, full]
        if part is not None:
            if row == 0:
                from_left, from_right = full | part & (x > 0), full | part & (x == 3)
                on_right = [full | part & inner, part & inner]
            else:
                from_left, from_right = full | part & (x == 0), full | part & (x < 3)
                on_left = [part & inner, full | part & inner]
        for t in range(2):
            here = (row, sl, t)
            arrived(from_left, here)
            if on_right[t] is not None:
                send(on_right[t], here, here, ss_x.at[phase, 4 + t], p.right)
            send(gathers, here, (1, sl, t), ss_c.at[sl, t], p.twin)
            here = (row, sr, t)
            arrived(from_right, here)
            if on_left[t] is not None:
                send(on_left[t], here, here, ss_x.at[phase, 6 + t], p.left)
            send(gathers, here, (1, sr, t), ss_c.at[sr, t], p.twin)

    def end(phase, row, other):
        full, part, gathers = modes(row, other)
        so = (p.other if other else p.own) + p.xo
        got = full
        if part is not None:
            got = full | part & ((x >= 2) if row == 0 else (x < 2))
        for t in range(2):
            here = (row, so, t)
            arrived(got, here)
            send(gathers, here, (1, so, t), ss_c.at[so, t], p.twin)

    def twin_sent(slots):
        for slot in slots:
            for t in range(2):
                arrived(s >= 1, (1, slot, t))

    def block_mask(row, slot):
        pos = ((s - row) * 8 + slot) * TOK + lax.broadcasted_iota(jnp.int32, (TOK, DH), 0)
        starts, ends = bounds[0:1, :], bounds[1:2, :]
        return jnp.where((pos >= starts) & (pos < ends), 0.0, -BIG).astype(jnp.bfloat16)

    def masks(blocks):
        for i, (row, slot) in enumerate(blocks):
            km[i * TOK:(i + 1) * TOK, :] = block_mask(row, slot)

    def one_head(j, blocks, first, last):
        width = len(blocks) * TOK
        lanes = pl.ds(pl.multiple_of(j * DH, DH), DH)
        keys = jnp.concatenate([kv[row, slot, 0, :, lanes] for row, slot in blocks], axis=0)
        keys = jnp.concatenate([keys, km[0:width, :]], axis=1)
        values = jnp.concatenate([kv[row, slot, 1, :, lanes] for row, slot in blocks], axis=0)
        values = jnp.concatenate([values, jnp.ones((width, DH), jnp.bfloat16)], axis=1)
        for part in range(ROWS // CHUNK):
            rows = pl.ds(part * CHUNK, CHUNK)
            scores = lax.dot_general(
                qa[j, rows, :], keys, (((1,), (1,)), ((), ())), preferred_element_type=jnp.float32
            )
            if first:
                token = lax.broadcasted_iota(jnp.int32, (CHUNK, width), 0) & (TOK - 1)
                key = lax.broadcasted_iota(jnp.int32, (CHUNK, width), 1)
                scores = jnp.where(key <= token, scores, -BIG)
            best = jnp.broadcast_to(jnp.max(scores, axis=1, keepdims=True), (CHUNK, DH))
            if not first:
                old = top[j, rows, :]
                best = jnp.maximum(best, old)
            weights = jnp.exp2((scores - spread(best, width)) * RATE).astype(jnp.bfloat16)
            both = jnp.dot(weights, values, preferred_element_type=jnp.float32)
            mixed, total = both[:, :DH], both[:, DH:]
            if not first:
                factor = jnp.exp2((old - best) * RATE)
                mixed = mixed + acc[j, rows, :] * factor
                total = total + tot[j, rows, :] * factor
            if last:
                done = (mixed / total).astype(jnp.bfloat16)
                for g in range(CHUNK // TOK):
                    column = (j * GROUP + part * (CHUNK // TOK) + g) * DH
                    out[:, pl.ds(pl.multiple_of(column, DH), DH)] = done[g * TOK:(g + 1) * TOK]
            else:
                top[j, rows, :] = best
                acc[j, rows, :] = mixed
                tot[j, rows, :] = total
        if last:
            columns = pl.ds(pl.multiple_of(j * GROUP * DH, DH), GROUP * DH)
            pltpu.make_async_copy(out.at[:, columns], o_hbm.at[:, columns], out_sem.at[j]).start()

    def attend(blocks, lo=0, hi=KVH, first=False, last=False):
        if lo == 0:
            masks(blocks)

        def some_heads(turn, carry):
            for j in range(UNROLL):
                one_head(lo + turn * UNROLL + j, blocks, first, last)
            return carry

        lax.fori_loop(0, (hi - lo) // UNROLL, some_heads, 0)

    far = p.other + x
    wanted = (core == 1) | (p.z == 0)
    mine = (k_hbm, v_hbm)
    for t in range(2):
        send(p.has_later, mine[t], (2, h, t), ss_y.at[0, t], p.later)
        begin(0, 0, False, t, mine[t])
    crosses = p.y == 3
    exchange = [send(None, mine[t], (0, h, t), ss_z.at[t], p.far, p.y != 3) for t in range(2)]


    lens = jnp.concatenate([len_ref[...], jnp.zeros((1, DH - len_ref.shape[1]), jnp.int32)], axis=1)
    lens = jnp.broadcast_to(lens, (8, DH))
    lane = lax.broadcasted_iota(jnp.int32, (8, DH), 1)
    ends = lens
    for step in (1, 2, 4, 8, 16, 32, 64):
        ends = ends + jnp.where(lane >= step, pltpu.roll(ends, step, 1), 0)
    bounds[0:1, :] = (ends - lens)[0:1]
    bounds[1:2, :] = ends[0:1]
    pos = (s * 8 + h) * TOK + lax.broadcasted_iota(jnp.int32, (TOK, DH), 0)
    member = jnp.where((pos >= bounds[0:1, :]) & (pos < bounds[1:2, :]), 1.0, 0.0).astype(jnp.bfloat16)
    loads[2].wait()

    def arrange(j, carry):
        for g in range(GROUP):
            column = pl.multiple_of((j * GROUP + g) * DH, DH)
            qa[j, g * TOK:(g + 1) * TOK, 0:DH] = q_raw[:, pl.ds(column, DH)]
            qa[j, g * TOK:(g + 1) * TOK, DH:2 * DH] = member
        return carry

    lax.fori_loop(0, KVH, arrange, 0)

    loads[0].wait()
    loads[1].wait()
    attend([(0, h)], first=True)

    @pl.when(crosses)
    def _():
        for t in range(2):
            when(p.has_later, sends[SHIFT[t]][1].wait_send)
        for copy in exchange:
            copy.start()

    middle(0, 0, False)
    for t in range(2):
        arrived(p.has_before, (2, h, t))
        begin(1, 2, False, t)
    end(0, 0, False)
    middle(1, 2, False)
    for t in range(2):
        arrived(None, (0, far, t))
        send(p.has_later & wanted, (0, far, t), (2, far, t), ss_y.at[1, t], p.later)
        begin(2, 0, True, t)
    end(1, 2, False)

    def mixed_row(other_x):
        return jnp.where(other_x < x, 0, 2)

    own, other = p.own, p.other
    mixed = [(mixed_row(d), own + d) for d in (p.xl, p.xr, p.xo)] + [(2, h)]
    before = [(1, own + d) for d in range(4)]
    attend(mixed, 0, 4)
    attend(mixed, 4, 8)
    middle(2, 0, True)
    for t in range(2):
        arrived(p.has_before & wanted, (2, far, t))
        begin(3, 2, True, t)
    twin_sent([own + d for d in range(4)])
    attend(before, 0, 4)
    end(2, 0, True)
    attend(before, 4, 8)

    late_both = (core == 0) & (p.z == 0)
    row_b = jnp.where(p.z == 0, 2, 0)
    first_row = jnp.where((core == 0) & (p.z == 1), row_b, 1)
    second_row = jnp.where((core == 0) & (p.z == 1), 1, row_b)
    order = [x, p.xl, p.xr, p.xo]
    plain = [(first_row, d) for d in order] + [(second_row, d) for d in order]
    paired = [(row, d) for d in order for row in (first_row, second_row)]
    todo = [
        (jnp.where(late_both, a, c), other + jnp.where(late_both, b, d))
        for (a, b), (c, d) in zip(paired, plain)
    ]


    for t in range(2):
        arrived(s >= 1, (1, far, t))
    early = (core == 1) & (s >= 1)
    for d in order[1:]:
        for t in range(2):
            arrived(early, (1, other + d, t))
    attend(todo[0:2])
    middle(3, 2, True)
    late = (core == 0) & (s >= 1)
    for d in order[1:3]:
        for t in range(2):
            arrived(late, (1, other + d, t))
    attend(todo[2:4])
    attend(todo[4:6])
    end(3, 2, True)
    for t in range(2):
        arrived(late, (1, other + p.xo, t))
    attend(todo[6:8], last=True)

    for i, (cond, copy) in enumerate(sends):
        if i in SHIFT:
            cond = cond & jnp.logical_not(crosses)
        when(cond, copy.wait_send)
    for j in range(KVH):
        columns = pl.ds(j * GROUP * DH, GROUP * DH)
        pltpu.make_async_copy(out.at[:, columns], o_hbm.at[:, columns], out_sem.at[j]).wait()


CHUNK = 256
UNROLL = 4
SHIFT = (0, 4)


def per_device(queries, keys, values, lengths):
    tok = queries.shape[0]
    f32, bf16, dma = jnp.float32, jnp.bfloat16, pltpu.SemaphoreType.DMA
    return pl.pallas_call(
        kernel,
        out_shape=jax.ShapeDtypeStruct(queries.shape, bf16),
        in_specs=[pl.BlockSpec(memory_space=pl.ANY)] * 3 + [pl.BlockSpec(memory_space=pltpu.VMEM)],
        out_specs=pl.BlockSpec(memory_space=pl.ANY),
        scratch_shapes=[
            pltpu.VMEM((3, 8, 2, tok, KVH * DH), bf16),
            pltpu.VMEM((tok, H * DH), bf16),
            pltpu.VMEM((KVH, ROWS, 2 * DH), bf16),
            pltpu.VMEM((4 * tok, DH), bf16),
            pltpu.VMEM((KVH, ROWS, DH), f32),
            pltpu.VMEM((KVH, ROWS, DH), f32),
            pltpu.VMEM((KVH, ROWS, DH), f32),
            pltpu.VMEM((tok, H * DH), bf16),
            pltpu.VMEM((8, DH), jnp.int32),
            dma((3,)), dma((KVH,)), dma((4, 8)), dma((8, 2)), dma((2, 2)), dma((2,)), dma((3, 8, 2)),
        ],
        compiler_params=pltpu.CompilerParams(
            collective_id=0, has_side_effects=True, vmem_limit_bytes=56 << 20
        ),
        name="attend",
    )(queries, keys, values, lengths.reshape(1, -1))


def solution(mesh):
    spec = P(("seq", "head"), None)
    return jax.shard_map(
        per_device, mesh=mesh, in_specs=(spec, spec, spec, P()), out_specs=spec, check_vma=False
    )
```

```python
import functools
import math

import jax
import jax.numpy as jnp
from jax import lax
from jax.experimental import pallas as pl
from jax.experimental.pallas import tpu as pltpu
from jax.sharding import PartitionSpec as P

H, KVH, DH = 64, 8, 128
GROUP = H // KVH
TOK = 128
ROWS = GROUP * TOK
BIG = 1e30
RATE = math.log2(math.e) / math.sqrt(DH)
MESH = pl.DeviceIdType.MESH


class Place:
    def __init__(self):
        self.s, self.h = s, h = lax.axis_index("seq"), lax.axis_index("head")
        self.core = lax.rem(s, 2)
        self.x, self.y, self.z = lax.rem(h, 4), lax.rem(s // 2, 4), h // 4
        self.own, self.other = self.z * 4, 4 - self.z * 4
        self.xl, self.xr, self.xo = (lax.rem(self.x + d, 4) for d in (3, 1, 2))
        self.right, self.left = (s, self.own + self.xr), (s, self.own + self.xl)
        self.far = (s, self.other + self.x)
        self.twin = (s + 1 - 2 * self.core, h)
        self.later, self.before = (s + 2, h), (s - 2, h)
        self.has_later, self.has_before = s < 30, s >= 2


def when(cond, action):
    if cond is None:
        action()
    else:
        pl.when(cond)(action)


def spread(column, width):
    return jnp.concatenate([column] * (width // 128), axis=1)


def kernel(
    q_hbm, k_hbm, v_hbm, len_ref, o_hbm,
    kv, q_raw, qa, km, acc, top, tot, out, bounds,
    load_sem, out_sem, ss_x, ss_c, ss_y, ss_z, rs,
):
    p = Place()
    s, h, core, x = p.s, p.h, p.core, p.x
    loads = [
        pltpu.make_async_copy(k_hbm, kv.at[0, h, 0], load_sem.at[0]),
        pltpu.make_async_copy(v_hbm, kv.at[0, h, 1], load_sem.at[1]),
        pltpu.make_async_copy(q_hbm, q_raw, load_sem.at[2]),
    ]
    for load in loads:
        load.start()

    barrier = pltpu.get_barrier_semaphore()

    def greet(device):
        pl.semaphore_signal(barrier, inc=1, device_id=device, device_id_type=MESH)

    for device in (p.left, p.right, p.far, p.twin):
        greet(device)
    when(p.has_before, lambda: greet(p.before))
    when(p.has_later, lambda: greet(p.later))

    @pl.when(s < 2)
    def _():
        kv[2] = jnp.zeros(kv.shape[1:], kv.dtype)

    @pl.when(s == 0)
    def _():
        kv[1] = jnp.zeros(kv.shape[1:], kv.dtype)

    pl.semaphore_wait(barrier, 4 + p.has_before.astype(jnp.int32) + p.has_later.astype(jnp.int32))
    sends = []

    def send(cond, src, dst, sem, device, now=None):
        copy = pltpu.make_async_remote_copy(
            src_ref=src if not isinstance(src, tuple) else kv.at[src], dst_ref=kv.at[dst], send_sem=sem, recv_sem=rs.at[dst],
            device_id=device, device_id_type=MESH,
        )
        when(cond if now is None else now, copy.start)
        sends.append((cond, copy))
        return copy

    def arrived(cond, where):
        copy = pltpu.make_async_remote_copy(
            src_ref=kv.at[where], dst_ref=kv.at[where], send_sem=ss_z.at[0], recv_sem=rs.at[where],
            device_id=p.right, device_id_type=MESH,
        )
        when(cond, copy.wait_recv)

    def modes(row, other):
        gathers = core == row // 2
        on = (s >= 2) if row == 2 else (s >= 0)
        if other:
            return on & (gathers | (core == p.z)), None, on & gathers
        return on & gathers, on & jnp.logical_not(gathers), on & gathers

    def begin(phase, row, other, t, source=None):
        full, part, gathers = modes(row, other)
        slot = (p.other if other else p.own) + x
        to_right, to_left = full, full
        if part is not None:
            if row == 0:
                to_right, to_left = full | part & (x < 3), full | part & (x <= t)
            else:
                to_right, to_left = full | part & (x >= 2 + t), full | part & (x > 0)
        here = (row, slot, t)
        source = here if source is None else source
        send(to_right, source, here, ss_x.at[phase, t], p.right)
        send(to_left, source, here, ss_x.at[phase, 2 + t], p.left)
        send(gathers, source, (1, slot, t), ss_c.at[slot, t], p.twin)

    def middle(phase, row, other, t):
        full, part, gathers = modes(row, other)
        base = p.other if other else p.own
        sl, sr = base + p.xl, base + p.xr
        inner = (x == 1) | (x == 2)
        from_left, from_right, hand_on = full, full, full
        if part is not None:
            if row == 0:
                from_left, from_right = full | part & (x > 0), full | part & ((x == 3) | (x == 0) & (t == 1))
                hand_on = full | part & (inner if t == 0 else ~inner)
            else:
                from_left, from_right = full | part & ((x == 0) | (x == 3) & (t == 0)), full | part & (x < 3)
                hand_on = full | part & (~inner if t == 0 else inner)
        here = (row, sl, t)
        arrived(from_left, here)
        if t == 0:
            send(hand_on, here, here, ss_x.at[phase, 4], p.right)
        send(gathers, here, (1, sl, t), ss_c.at[sl, t], p.twin)
        here = (row, sr, t)
        arrived(from_right, here)
        if t == 1:
            send(hand_on, here, here, ss_x.at[phase, 5], p.left)
        send(gathers, here, (1, sr, t), ss_c.at[sr, t], p.twin)

    def end(phase, row, other):
        full, part, gathers = modes(row, other)
        so = (p.other if other else p.own) + p.xo
        got = full
        if part is not None:
            got = full | part & ((x >= 2) if row == 0 else (x < 2))
        for t in range(2):
            here = (row, so, t)
            arrived(got, here)
            send(gathers, here, (1, so, t), ss_c.at[so, t], p.twin)

    def block_mask(row, slot):
        pos = ((s - row) * 8 + slot) * TOK + lax.broadcasted_iota(jnp.int32, (TOK, DH), 0)
        starts, ends = bounds[0:1, :], bounds[1:2, :]
        return jnp.where((pos >= starts) & (pos < ends), 0.0, -BIG).astype(jnp.bfloat16)

    def masks(blocks):
        for i, (row, slot) in enumerate(blocks):
            km[i * TOK:(i + 1) * TOK, :] = block_mask(row, slot)

    def one_head(j, blocks, first, last):
        width = len(blocks) * TOK
        lanes = pl.ds(pl.multiple_of(j * DH, DH), DH)
        keys = jnp.concatenate([kv[row, slot, 0, :, lanes] for row, slot in blocks], axis=0)
        keys = jnp.concatenate([keys, km[0:width, :]], axis=1)
        values = jnp.concatenate([kv[row, slot, 1, :, lanes] for row, slot in blocks], axis=0)
        values = jnp.concatenate([values, jnp.ones((width, DH), jnp.bfloat16)], axis=1)
        for part in range(ROWS // CHUNK):
            rows = pl.ds(part * CHUNK, CHUNK)
            scores = lax.dot_general(
                qa[j, rows, :], keys, (((1,), (1,)), ((), ())), preferred_element_type=jnp.float32
            )
            if first:
                token = lax.broadcasted_iota(jnp.int32, (CHUNK, width), 0) & (TOK - 1)
                key = lax.broadcasted_iota(jnp.int32, (CHUNK, width), 1)
                scores = jnp.where(key <= token, scores, -BIG)
            best = jnp.broadcast_to(jnp.max(scores, axis=1, keepdims=True), (CHUNK, DH))
            if not first:
                old = top[j, rows, :]
                best = jnp.maximum(best, old)
            weights = jnp.exp2((scores - spread(best, width)) * RATE).astype(jnp.bfloat16)
            both = jnp.dot(weights, values, preferred_element_type=jnp.float32)
            mixed, total = both[:, :DH], both[:, DH:]
            if not first:
                factor = jnp.exp2((old - best) * RATE)
                mixed = mixed + acc[j, rows, :] * factor
                total = total + tot[j, rows, :] * factor
            if last:
                done = (mixed / total).astype(jnp.bfloat16)
                for g in range(CHUNK // TOK):
                    column = (j * GROUP + part * (CHUNK // TOK) + g) * DH
                    out[:, pl.ds(pl.multiple_of(column, DH), DH)] = done[g * TOK:(g + 1) * TOK]
            else:
                top[j, rows, :] = best
                acc[j, rows, :] = mixed
                tot[j, rows, :] = total
        if last:
            columns = pl.ds(pl.multiple_of(j * GROUP * DH, DH), GROUP * DH)
            pltpu.make_async_copy(out.at[:, columns], o_hbm.at[:, columns], out_sem.at[j]).start()

    def attend(blocks, lo=0, hi=KVH, first=False, last=False):
        if lo == 0:
            masks(blocks)

        def some_heads(turn, carry):
            for j in range(UNROLL):
                one_head(lo + turn * UNROLL + j, blocks, first, last)
            return carry

        lax.fori_loop(0, (hi - lo) // UNROLL, some_heads, 0)

    far = p.other + x
    wanted = (core == 1) | (p.z == 0)
    passes = [((core == 1) & (p.z == 1)) | ((p.z == 0) & ((p.y != 3) | (t == 1) & (s < 8))) for t in range(2)]
    mine = (k_hbm, v_hbm)
    for t in range(2):
        send(p.has_later, mine[t], (2, h, t), ss_y.at[0, t], p.later)
        begin(0, 0, False, t, mine[t])
    for t in range(2):
        send(None, mine[t], (0, h, t), ss_z.at[t], p.far)

    lens = jnp.concatenate([len_ref[...], jnp.zeros((1, DH - len_ref.shape[1]), jnp.int32)], axis=1)
    lens = jnp.broadcast_to(lens, (8, DH))
    lane = lax.broadcasted_iota(jnp.int32, (8, DH), 1)
    ends = lens
    for step in (1, 2, 4, 8, 16, 32, 64):
        ends = ends + jnp.where(lane >= step, pltpu.roll(ends, step, 1), 0)
    bounds[0:1, :] = (ends - lens)[0:1]
    bounds[1:2, :] = ends[0:1]
    pos = (s * 8 + h) * TOK + lax.broadcasted_iota(jnp.int32, (TOK, DH), 0)
    member = jnp.where((pos >= bounds[0:1, :]) & (pos < bounds[1:2, :]), 1.0, 0.0).astype(jnp.bfloat16)
    loads[2].wait()

    def arrange(j, carry):
        for g in range(GROUP):
            column = pl.multiple_of((j * GROUP + g) * DH, DH)
            qa[j, g * TOK:(g + 1) * TOK, 0:DH] = q_raw[:, pl.ds(column, DH)]
            qa[j, g * TOK:(g + 1) * TOK, DH:2 * DH] = member
        return carry

    lax.fori_loop(0, KVH, arrange, 0)

    loads[0].wait()
    loads[1].wait()
    attend([(0, h)], first=True)

    def mixed_row(other_x):
        return jnp.where(other_x < x, 0, 2)

    own, other = p.own, p.other
    mixed = [(mixed_row(d), own + d) for d in (p.xl, p.xr, p.xo)] + [(2, h)]
    before = [(1, own + d) for d in range(4)]
    late_both = (core == 0) & (p.z == 0)
    row_b = jnp.where(p.z == 0, 2, 0)
    first_row = jnp.where((core == 0) & (p.z == 1), row_b, 1)
    second_row = jnp.where((core == 0) & (p.z == 1), 1, row_b)
    order = [x, p.xl, p.xr, p.xo]
    plain = [(first_row, d) for d in order] + [(second_row, d) for d in order]
    paired = [(row, d) for d in order for row in (first_row, second_row)]
    todo = [
        (jnp.where(late_both, a, c), other + jnp.where(late_both, b, d))
        for (a, b), (c, d) in zip(paired, plain)
    ]


    early = (core == 1) & (s >= 1)
    late = (core == 0) & (s >= 1)

    def twin_sent(slot, cond):
        for t in range(2):
            arrived(cond, (1, slot, t))

    def from_shift(t):
        arrived(p.has_before, (2, h, t))
        begin(1, 2, False, t)
        send(p.has_before & (p.y == 0) & (p.z == 1) & ((t == 0) | (s >= 16)), (2, h, t), (2, h, t), ss_z.at[2 + t], p.far)

    def from_far(t):
        arrived(None, (0, far, t))
        send(p.has_later & passes[t], (0, far, t), (2, far, t), ss_y.at[1, t], p.later)
        begin(2, 0, True, t)

    def from_far_shift(t):
        arrived(p.has_before & wanted, (2, far, t))
        begin(3, 2, True, t)

    def row_before(lo, hi):
        if lo == 0:
            for d in range(4):
                twin_sent(own + d, s >= 1)
        attend(before, lo, hi)

    def left_over(i):
        if i == 0:
            twin_sent(far, s >= 1)
            for d in order[1:]:
                twin_sent(other + d, early)
        if i == 1:
            for d in order[1:3]:
                twin_sent(other + d, late)
        if i == 3:
            twin_sent(other + p.xo, late)
        attend(todo[2 * i:2 * i + 2], last=i == 3)

    middle(0, 0, False, 0)
    from_shift(0)
    middle(0, 0, False, 1)
    from_shift(1)
    end(0, 0, False)
    middle(1, 2, False, 0)
    from_far(0)
    middle(1, 2, False, 1)
    from_far(1)
    end(1, 2, False)
    attend(mixed, 0, 4)
    middle(2, 0, True, 0)
    middle(2, 0, True, 1)
    from_far_shift(0)
    from_far_shift(1)
    attend(mixed, 4, 8)
    row_before(0, 4)
    end(2, 0, True)
    row_before(4, 8)
    left_over(0)
    middle(3, 2, True, 0)
    middle(3, 2, True, 1)
    left_over(1)
    left_over(2)
    end(3, 2, True)
    left_over(3)
    for cond, copy in sends:
        when(cond, copy.wait_send)
    for j in range(KVH):
        columns = pl.ds(j * GROUP * DH, GROUP * DH)
        pltpu.make_async_copy(out.at[:, columns], o_hbm.at[:, columns], out_sem.at[j]).wait()


CHUNK = 256
UNROLL = 4


def per_device(queries, keys, values, lengths):
    tok = queries.shape[0]
    f32, bf16, dma = jnp.float32, jnp.bfloat16, pltpu.SemaphoreType.DMA
    return pl.pallas_call(
        kernel,
        out_shape=jax.ShapeDtypeStruct(queries.shape, bf16),
        in_specs=[pl.BlockSpec(memory_space=pl.ANY)] * 3 + [pl.BlockSpec(memory_space=pltpu.VMEM)],
        out_specs=pl.BlockSpec(memory_space=pl.ANY),
        scratch_shapes=[
            pltpu.VMEM((3, 8, 2, tok, KVH * DH), bf16),
            pltpu.VMEM((tok, H * DH), bf16),
            pltpu.VMEM((KVH, ROWS, 2 * DH), bf16),
            pltpu.VMEM((4 * tok, DH), bf16),
            pltpu.VMEM((KVH, ROWS, DH), f32),
            pltpu.VMEM((KVH, ROWS, DH), f32),
            pltpu.VMEM((KVH, ROWS, DH), f32),
            pltpu.VMEM((tok, H * DH), bf16),
            pltpu.VMEM((8, DH), jnp.int32),
            dma((3,)), dma((KVH,)), dma((4, 6)), dma((8, 2)), dma((2, 2)), dma((4,)), dma((3, 8, 2)),
        ],
        compiler_params=pltpu.CompilerParams(
            collective_id=0, has_side_effects=True, vmem_limit_bytes=56 << 20
        ),
        name="attend",
    )(queries, keys, values, lengths.reshape(1, -1))


def solution(mesh):
    spec = P(("seq", "head"), None)
    return jax.shard_map(
        per_device, mesh=mesh, in_specs=(spec, spec, spec, P()), out_specs=spec, check_vma=False
    )
```

```python
import functools
import math

import jax
import jax.numpy as jnp
from jax import lax
from jax.experimental import pallas as pl
from jax.experimental.pallas import tpu as pltpu
from jax.sharding import PartitionSpec as P

H, KVH, DH = 64, 8, 128
GROUP = H // KVH
TOK = 128
ROWS = GROUP * TOK
BIG = 1e30
RATE = math.log2(math.e) / math.sqrt(DH)
MESH = pl.DeviceIdType.MESH


class Place:
    def __init__(self):
        self.s, self.h = s, h = lax.axis_index("seq"), lax.axis_index("head")
        self.core = lax.rem(s, 2)
        self.x, self.y, self.z = lax.rem(h, 4), lax.rem(s // 2, 4), h // 4
        self.own, self.other = self.z * 4, 4 - self.z * 4
        self.xl, self.xr, self.xo = (lax.rem(self.x + d, 4) for d in (3, 1, 2))
        self.right, self.left = (s, self.own + self.xr), (s, self.own + self.xl)
        self.far = (s, self.other + self.x)
        self.twin = (s + 1 - 2 * self.core, h)
        self.later, self.before = (s + 2, h), (s - 2, h)
        self.has_later, self.has_before = s < 30, s >= 2


def when(cond, action):
    if cond is None:
        action()
    else:
        pl.when(cond)(action)


def spread(column, width):
    return jnp.concatenate([column] * (width // 128), axis=1)


def kernel(
    q_hbm, k_hbm, v_hbm, len_ref, o_hbm,
    kv, q_raw, qa, km, acc, top, tot, out, bounds,
    load_sem, out_sem, ss_x, ss_c, ss_y, ss_z, rs,
):
    p = Place()
    s, h, core, x = p.s, p.h, p.core, p.x
    loads = [
        pltpu.make_async_copy(k_hbm, kv.at[0, h, 0], load_sem.at[0]),
        pltpu.make_async_copy(v_hbm, kv.at[0, h, 1], load_sem.at[1]),
        pltpu.make_async_copy(q_hbm, q_raw, load_sem.at[2]),
    ]
    for load in loads:
        load.start()

    barrier = pltpu.get_barrier_semaphore()

    def greet(device):
        pl.semaphore_signal(barrier, inc=1, device_id=device, device_id_type=MESH)

    for device in (p.left, p.right, p.far, p.twin):
        greet(device)
    when(p.has_before, lambda: greet(p.before))
    when(p.has_later, lambda: greet(p.later))

    @pl.when(s < 2)
    def _():
        kv[2] = jnp.zeros(kv.shape[1:], kv.dtype)

    @pl.when(s == 0)
    def _():
        kv[1] = jnp.zeros(kv.shape[1:], kv.dtype)

    pl.semaphore_wait(barrier, 4 + p.has_before.astype(jnp.int32) + p.has_later.astype(jnp.int32))
    sends = []

    def send(cond, src, dst, sem, device, now=None):
        copy = pltpu.make_async_remote_copy(
            src_ref=src if not isinstance(src, tuple) else kv.at[src], dst_ref=kv.at[dst], send_sem=sem, recv_sem=rs.at[dst],
            device_id=device, device_id_type=MESH,
        )
        when(cond if now is None else now, copy.start)
        sends.append((cond, copy))
        return copy

    def arrived(cond, where):
        copy = pltpu.make_async_remote_copy(
            src_ref=kv.at[where], dst_ref=kv.at[where], send_sem=ss_z.at[0], recv_sem=rs.at[where],
            device_id=p.right, device_id_type=MESH,
        )
        when(cond, copy.wait_recv)

    def modes(row, other):
        gathers = core == row // 2
        on = (s >= 2) if row == 2 else (s >= 0)
        if other:
            return on & (gathers | (core == p.z)), None, on & gathers
        return on & gathers, on & jnp.logical_not(gathers), on & gathers

    def begin(phase, row, other, t, source=None):
        full, part, gathers = modes(row, other)
        slot = (p.other if other else p.own) + x
        to_right, to_left = full, full
        if part is not None:
            if row == 0:
                to_right, to_left = full | part & (x < 3), full | part & (x <= t)
            else:
                to_right, to_left = full | part & (x >= 2 + t), full | part & (x > 0)
        here = (row, slot, t)
        source = here if source is None else source
        send(to_right, source, here, ss_x.at[phase, t], p.right)
        send(to_left, source, here, ss_x.at[phase, 2 + t], p.left)
        send(gathers, source, (1, slot, t), ss_c.at[slot, t], p.twin)

    def middle(phase, row, other, t):
        full, part, gathers = modes(row, other)
        base = p.other if other else p.own
        sl, sr = base + p.xl, base + p.xr
        inner = (x == 1) | (x == 2)
        from_left, from_right, hand_on = full, full, full
        if part is not None:
            if row == 0:
                from_left, from_right = full | part & (x > 0), full | part & ((x == 3) | (x == 0) & (t == 1))
                hand_on = full | part & (inner if t == 0 else ~inner)
            else:
                from_left, from_right = full | part & ((x == 0) | (x == 3) & (t == 0)), full | part & (x < 3)
                hand_on = full | part & (~inner if t == 0 else inner)
        here = (row, sl, t)
        arrived(from_left, here)
        if t == 0:
            send(hand_on, here, here, ss_x.at[phase, 4], p.right)
        send(gathers, here, (1, sl, t), ss_c.at[sl, t], p.twin)
        here = (row, sr, t)
        arrived(from_right, here)
        if t == 1:
            send(hand_on, here, here, ss_x.at[phase, 5], p.left)
        send(gathers, here, (1, sr, t), ss_c.at[sr, t], p.twin)

    def end(phase, row, other):
        full, part, gathers = modes(row, other)
        so = (p.other if other else p.own) + p.xo
        got = full
        if part is not None:
            got = full | part & ((x >= 2) if row == 0 else (x < 2))
        for t in range(2):
            here = (row, so, t)
            arrived(got, here)
            send(gathers, here, (1, so, t), ss_c.at[so, t], p.twin)

    def block_mask(row, slot):
        pos = ((s - row) * 8 + slot) * TOK + lax.broadcasted_iota(jnp.int32, (TOK, DH), 0)
        starts, ends = bounds[0:1, :], bounds[1:2, :]
        return jnp.where((pos >= starts) & (pos < ends), 0.0, -BIG).astype(jnp.bfloat16)

    def masks(blocks):
        for i, (row, slot) in enumerate(blocks):
            km[i * TOK:(i + 1) * TOK, :] = block_mask(row, slot)

    def one_head(j, blocks, first, last):
        width = len(blocks) * TOK
        lanes = pl.ds(pl.multiple_of(j * DH, DH), DH)
        keys = jnp.concatenate([kv[row, slot, 0, :, lanes] for row, slot in blocks], axis=0)
        keys = jnp.concatenate([keys, km[0:width, :]], axis=1)
        values = jnp.concatenate([kv[row, slot, 1, :, lanes] for row, slot in blocks], axis=0)
        values = jnp.concatenate([values, jnp.ones((width, DH), jnp.bfloat16)], axis=1)
        for part in range(ROWS // CHUNK):
            rows = pl.ds(part * CHUNK, CHUNK)
            scores = lax.dot_general(
                qa[j, rows, :], keys, (((1,), (1,)), ((), ())), preferred_element_type=jnp.float32
            )
            if first:
                token = lax.broadcasted_iota(jnp.int32, (CHUNK, width), 0) & (TOK - 1)
                key = lax.broadcasted_iota(jnp.int32, (CHUNK, width), 1)
                scores = jnp.where(key <= token, scores, -BIG)
            best = jnp.broadcast_to(jnp.max(scores, axis=1, keepdims=True), (CHUNK, DH))
            if not first:
                old = top[j, rows, :]
                best = jnp.maximum(best, old)
            weights = jnp.exp2((scores - spread(best, width)) * RATE).astype(jnp.bfloat16)
            both = jnp.dot(weights, values, preferred_element_type=jnp.float32)
            mixed, total = both[:, :DH], both[:, DH:]
            if not first:
                factor = jnp.exp2((old - best) * RATE)
                mixed = mixed + acc[j, rows, :] * factor
                total = total + tot[j, rows, :] * factor
            if last:
                done = (mixed / total).astype(jnp.bfloat16)
                for g in range(CHUNK // TOK):
                    column = (j * GROUP + part * (CHUNK // TOK) + g) * DH
                    out[:, pl.ds(pl.multiple_of(column, DH), DH)] = done[g * TOK:(g + 1) * TOK]
            else:
                top[j, rows, :] = best
                acc[j, rows, :] = mixed
                tot[j, rows, :] = total
        if last:
            columns = pl.ds(pl.multiple_of(j * GROUP * DH, DH), GROUP * DH)
            pltpu.make_async_copy(out.at[:, columns], o_hbm.at[:, columns], out_sem.at[j]).start()

    def attend(blocks, lo=0, hi=KVH, first=False, last=False):
        if lo == 0:
            masks(blocks)

        def some_heads(turn, carry):
            for j in range(UNROLL):
                one_head(lo + turn * UNROLL + j, blocks, first, last)
            return carry

        lax.fori_loop(0, (hi - lo) // UNROLL, some_heads, 0)

    far = p.other + x
    wanted = (core == 1) | (p.z == 0)
    passes = [((core == 1) & (p.z == 1)) | ((p.z == 0) & ((p.y != 3) | (t == 1) & (s < 8))) for t in range(2)]
    mine = (k_hbm, v_hbm)
    for t in range(2):
        send(p.has_later, mine[t], (2, h, t), ss_y.at[0, t], p.later)
        begin(0, 0, False, t, mine[t])
    for t in range(2):
        send(None, mine[t], (0, h, t), ss_z.at[t], p.far)

    lens = jnp.concatenate([len_ref[...], jnp.zeros((1, DH - len_ref.shape[1]), jnp.int32)], axis=1)
    lens = jnp.broadcast_to(lens, (8, DH))
    lane = lax.broadcasted_iota(jnp.int32, (8, DH), 1)
    ends = lens
    for step in (1, 2, 4, 8, 16, 32, 64):
        ends = ends + jnp.where(lane >= step, pltpu.roll(ends, step, 1), 0)
    bounds[0:1, :] = (ends - lens)[0:1]
    bounds[1:2, :] = ends[0:1]
    pos = (s * 8 + h) * TOK + lax.broadcasted_iota(jnp.int32, (TOK, DH), 0)
    member = jnp.where((pos >= bounds[0:1, :]) & (pos < bounds[1:2, :]), 1.0, 0.0).astype(jnp.bfloat16)
    loads[2].wait()

    def arrange(j, carry):
        for g in range(GROUP):
            column = pl.multiple_of((j * GROUP + g) * DH, DH)
            qa[j, g * TOK:(g + 1) * TOK, 0:DH] = q_raw[:, pl.ds(column, DH)]
            qa[j, g * TOK:(g + 1) * TOK, DH:2 * DH] = member
        return carry

    lax.fori_loop(0, KVH, arrange, 0)

    loads[0].wait()
    loads[1].wait()
    attend([(0, h)], first=True)

    def mixed_row(other_x):
        return jnp.where(other_x < x, 0, 2)

    own, other = p.own, p.other
    mixed = [(mixed_row(d), own + d) for d in (p.xl, p.xr, p.xo)] + [(2, h)]
    before = [(1, own + d) for d in range(4)]
    late_both = (core == 0) & (p.z == 0)
    row_b = jnp.where(p.z == 0, 2, 0)
    first_row = jnp.where((core == 0) & (p.z == 1), row_b, 1)
    second_row = jnp.where((core == 0) & (p.z == 1), 1, row_b)
    order = [x, p.xl, p.xr, p.xo]
    plain = [(first_row, d) for d in order] + [(second_row, d) for d in order]
    paired = [(row, d) for d in order for row in (first_row, second_row)]
    todo = [
        (jnp.where(late_both, a, c), other + jnp.where(late_both, b, d))
        for (a, b), (c, d) in zip(paired, plain)
    ]


    early = (core == 1) & (s >= 1)
    late = (core == 0) & (s >= 1)

    def twin_sent(slot, cond):
        for t in range(2):
            arrived(cond, (1, slot, t))

    def from_shift(t):
        arrived(p.has_before, (2, h, t))
        begin(1, 2, False, t)
        send(p.has_before & (p.y == 0) & (p.z == 1) & ((t == 0) | (s >= 16)), (2, h, t), (2, h, t), ss_z.at[2 + t], p.far)

    def from_far(t):
        arrived(None, (0, far, t))
        send(p.has_later & passes[t], (0, far, t), (2, far, t), ss_y.at[1, t], p.later)
        begin(2, 0, True, t)

    def from_far_shift(t):
        arrived(p.has_before & wanted, (2, far, t))
        begin(3, 2, True, t)

    def row_before(lo, hi):
        if lo == 0:
            for d in range(4):
                twin_sent(own + d, s >= 1)
        attend(before, lo, hi)

    def left_over(i):
        if i == 0:
            twin_sent(far, s >= 1)
            for d in order[1:]:
                twin_sent(other + d, early)
        if i == 1:
            for d in order[1:3]:
                twin_sent(other + d, late)
        if i == 3:
            twin_sent(other + p.xo, late)
        attend(todo[2 * i:2 * i + 2], last=i == 3)

    middle(0, 0, False, 0)
    from_shift(0)
    middle(0, 0, False, 1)
    from_shift(1)
    end(0, 0, False)
    middle(1, 2, False, 0)
    from_far(0)
    middle(1, 2, False, 1)
    from_far(1)
    end(1, 2, False)
    attend(mixed, 0, 4)
    middle(2, 0, True, 0)
    middle(2, 0, True, 1)
    from_far_shift(0)
    from_far_shift(1)
    attend(mixed, 4, 8)
    row_before(0, 4)
    end(2, 0, True)
    row_before(4, 8)
    left_over(0)
    middle(3, 2, True, 0)
    middle(3, 2, True, 1)
    left_over(1)
    left_over(2)
    end(3, 2, True)
    left_over(3)
    for cond, copy in sends:
        when(cond, copy.wait_send)
    for j in range(KVH):
        columns = pl.ds(j * GROUP * DH, GROUP * DH)
        pltpu.make_async_copy(out.at[:, columns], o_hbm.at[:, columns], out_sem.at[j]).wait()


CHUNK = 512
UNROLL = 4


def per_device(queries, keys, values, lengths):
    tok = queries.shape[0]
    f32, bf16, dma = jnp.float32, jnp.bfloat16, pltpu.SemaphoreType.DMA
    return pl.pallas_call(
        kernel,
        out_shape=jax.ShapeDtypeStruct(queries.shape, bf16),
        in_specs=[pl.BlockSpec(memory_space=pl.ANY)] * 3 + [pl.BlockSpec(memory_space=pltpu.VMEM)],
        out_specs=pl.BlockSpec(memory_space=pl.ANY),
        scratch_shapes=[
            pltpu.VMEM((3, 8, 2, tok, KVH * DH), bf16),
            pltpu.VMEM((tok, H * DH), bf16),
            pltpu.VMEM((KVH, ROWS, 2 * DH), bf16),
            pltpu.VMEM((4 * tok, DH), bf16),
            pltpu.VMEM((KVH, ROWS, DH), f32),
            pltpu.VMEM((KVH, ROWS, DH), f32),
            pltpu.VMEM((KVH, ROWS, DH), f32),
            pltpu.VMEM((tok, H * DH), bf16),
            pltpu.VMEM((8, DH), jnp.int32),
            dma((3,)), dma((KVH,)), dma((4, 6)), dma((8, 2)), dma((2, 2)), dma((4,)), dma((3, 8, 2)),
        ],
        compiler_params=pltpu.CompilerParams(
            collective_id=0, has_side_effects=True, vmem_limit_bytes=56 << 20
        ),
        name="attend",
    )(queries, keys, values, lengths.reshape(1, -1))


def solution(mesh):
    spec = P(("seq", "head"), None)
    return jax.shard_map(
        per_device, mesh=mesh, in_specs=(spec, spec, spec, P()), out_specs=spec, check_vma=False
    )
```
